32 devices in a mesh: groups: 2 (over y), freq: 4 (over z), src: 2 (over x), vp: 2 (over core).
Axes of the slice: x: 2, y: 2, z: 4, core: 2. Of those that a mesh axis runs over, the one named last changes fastest.
Arguments:
- focus_direct: bfloat16 [4, 2, 192, 8192], P('freq', None, ('groups', 'vp'), 'src'), parts along dimension 2, may hold values from -6 to 6
- u_factors: bfloat16 [4, 32, 2, 32, 2048], P('freq', 'src'), may hold values from -0.1875 to 0.1875
- v_factors: bfloat16 [4, 8, 2, 32, 8192], P('freq', None, None, None, 'src'), may hold values from -0.375 to 0.375
- tile_ranks: int32 [4, 8, 32], P('freq', None, 'src'), may hold values from 16 to 32
- onset_rec: int32 [192, 2048], P(('groups', 'vp'), 'src'), parts along dimension 0, may hold values from 64 to 191
- onset_src: int32 [192, 8192], P(('groups', 'vp'), 'src'), parts along dimension 0, may hold values from 64 to 191
Outputs:
- focus_plus: bfloat16 [4, 2, 192, 8192], P('freq', None, ('groups', 'vp'), 'src'), parts along dimension 2
- focus_minus: bfloat16 [4, 2, 192, 2048], P('freq', None, ('groups', 'vp'), 'src'), parts along dimension 2
The draws below stay inside these ranges and needn't reach their ends.
There are 2 independent parts, one for each index of `groups`. The reference program is written for one: setup_inputs(seed, part) draws one part's arguments, and reference() takes and returns one part's arrays. A program takes and returns all parts, laid end to end along the dimension named above; an argument that names none is the same for every part. Nothing has to cross between parts.
All inputs are finite; a program needn't handle non-finite values.
Results may differ from the reference program's by a relative error of at most 0.018.
Values may be sent and summed in bfloat16 or wider, within the bound.
A program may use at most 128 MiB of HBM per device.

```python
import math
import jax
import jax.numpy as jnp
from jax import lax

NR = 2048
NS = 8192
TILE = 256
RANK = 32
NT = 256
FLO = 8
ITERS = 2
NF = 4
VP = 96
RT = 8
CT = 32


def with_ends(values, own_key, least, top_value):
    shape = values.shape
    index_at = [jax.random.randint(jax.random.fold_in(own_key, axis), (), 0, shape[axis]) for axis in range(len(shape))]
    values = values.at[tuple(index_at)].set(least)
    longest = shape.index(max(shape))
    index_at[longest] = (index_at[longest] + 1) % shape[longest]
    return values.at[tuple(index_at)].set(top_value)


def steps_of(rng, dims, cuts, low, high):
    def one(position, shards_of):
        heights = jax.random.uniform(jax.random.fold_in(jax.random.fold_in(rng, 6), position), (shards_of,), jnp.float32, low / len(cuts), high / len(cuts))
        return jnp.repeat(jnp.exp(heights), dims[position] // shards_of).reshape((-1,) + (1,) * (len(dims) - position - 1))

    factor_of = one(*cuts[0])
    for cut in cuts[1:]:
        factor_of = factor_of * one(*cut)
    return factor_of


def centred(stream_key, dims, width, reach, split=(), kind=jnp.bfloat16):
    values = jax.random.normal(stream_key, dims, jnp.float32) * width
    if len(split) > 0:
        values = steps_of(stream_key, dims, split, -0.22, 0.18) * values
    return jnp.clip(values, min=-reach, max=reach).astype(kind)


def setup_inputs(seed: int = 0, part: int = 0) -> dict:
    splits = jax.random.split(jax.random.key(seed), 7)
    part_splits = jax.random.split(jax.random.fold_in(splits[6], part), 7)
    return {
        "focus_direct": centred(part_splits[0], (NF, 2, VP, NS), 1.0, 6.0, ((0, 4), (2, 2), (3, 2))),
        "u_factors": centred(splits[1], (NF, CT, 2, RANK, NR), (RANK * NS // TILE) ** -0.5, 0.1875, ((0, 4), (1, 2))),
        "v_factors": centred(splits[2], (NF, RT, 2, RANK, NS), TILE ** -0.5, 0.375, ((0, 4), (4, 2))),
        "tile_ranks": with_ends(jax.random.randint(splits[3], (NF, RT, CT), RANK // 2, RANK + 1), jax.random.fold_in(splits[3], 1), RANK // 2, RANK).astype(jnp.int32),
        "onset_rec": with_ends(jax.random.randint(part_splits[4], (VP, NR), NT // 4, 3 * NT // 4), jax.random.fold_in(part_splits[4], 1), NT // 4, (3 * NT // 4) - 1).astype(jnp.int32),
        "onset_src": with_ends(jax.random.randint(part_splits[5], (VP, NS), NT // 4, 3 * NT // 4), jax.random.fold_in(part_splits[5], 1), NT // 4, (3 * NT // 4) - 1).astype(jnp.int32),
    }


def make_tables(count):
    index = FLO + jnp.arange(count, dtype=jnp.int32)
    sample = jnp.arange(NT, dtype=jnp.int32)
    phase = ((index[:, None] * sample[None, :]) % NT).astype(jnp.float32) * (2.0 * math.pi / NT)
    cosine = jnp.cos(phase)
    sine = jnp.sin(phase)
    inverse = jnp.stack([cosine, -sine]) * (2.0 / NT)
    forward = jnp.stack([cosine, -sine])
    return inverse, forward


def window_trace(spectrum, onset, inverse, forward):
    signal = jnp.einsum("fcm,cft->mt", spectrum, inverse, precision=lax.Precision.HIGHEST)
    keep = jnp.arange(NT, dtype=jnp.int32)[None, :] < onset[:, None]
    signal = jnp.where(keep, signal, jnp.zeros_like(signal))
    return jnp.einsum("mt,cft->fcm", signal, forward, precision=lax.Precision.HIGHEST)


def window(spectrum, onset):
    inverse, forward = make_tables(spectrum.shape[0])
    moved = jnp.moveaxis(spectrum, 2, 0)
    result = lax.map(lambda pair: window_trace(pair[0], pair[1], inverse, forward), (moved, onset))
    return jnp.moveaxis(result, 0, 2)


def rank_mask(ranks):
    return (jnp.arange(RANK, dtype=jnp.int32)[None, None, :] < ranks[:, :, None])[:, None]


def round_half(values):
    rounded = values.astype(jnp.bfloat16)
    rounded = lax.optimization_barrier(rounded)
    return rounded.astype(jnp.float32)


def forward_one(args):
    u_fac, v_fac, ranks, focus = args
    source = focus.astype(jnp.float32).reshape(2, VP, CT, TILE)
    v_tiles = v_fac.astype(jnp.float32).reshape(RT, 2, RANK, CT, TILE)
    u_tiles = u_fac.astype(jnp.float32).reshape(CT, 2, RANK, RT, TILE)
    z_real = jnp.einsum("irjt,vjt->ivjr", v_tiles[:, 0], source[0]) + jnp.einsum("irjt,vjt->ivjr", v_tiles[:, 1], source[1])
    z_imag = jnp.einsum("irjt,vjt->ivjr", v_tiles[:, 0], source[1]) - jnp.einsum("irjt,vjt->ivjr", v_tiles[:, 1], source[0])
    mask = rank_mask(ranks)
    z_real = round_half(jnp.where(mask, z_real, 0.0))
    z_imag = round_half(jnp.where(mask, z_imag, 0.0))
    y_real = jnp.einsum("jrit,ivjr->vit", u_tiles[:, 0], z_real) - jnp.einsum("jrit,ivjr->vit", u_tiles[:, 1], z_imag)
    y_imag = jnp.einsum("jrit,ivjr->vit", u_tiles[:, 0], z_imag) + jnp.einsum("jrit,ivjr->vit", u_tiles[:, 1], z_real)
    return jnp.stack([y_real.reshape(VP, NR), y_imag.reshape(VP, NR)])


def adjoint_one(args):
    u_fac, v_fac, ranks, focus = args
    receiver = focus.astype(jnp.float32).reshape(2, VP, RT, TILE)
    v_tiles = v_fac.astype(jnp.float32).reshape(RT, 2, RANK, CT, TILE)
    u_tiles = u_fac.astype(jnp.float32).reshape(CT, 2, RANK, RT, TILE)
    w_real = jnp.einsum("jrit,vit->ivjr", u_tiles[:, 0], receiver[0]) + jnp.einsum("jrit,vit->ivjr", u_tiles[:, 1], receiver[1])
    w_imag = jnp.einsum("jrit,vit->ivjr", u_tiles[:, 0], receiver[1]) - jnp.einsum("jrit,vit->ivjr", u_tiles[:, 1], receiver[0])
    mask = rank_mask(ranks)
    w_real = round_half(jnp.where(mask, w_real, 0.0))
    w_imag = round_half(jnp.where(mask, w_imag, 0.0))
    x_real = jnp.einsum("irjt,ivjr->vjt", v_tiles[:, 0], w_real) - jnp.einsum("irjt,ivjr->vjt", v_tiles[:, 1], w_imag)
    x_imag = jnp.einsum("irjt,ivjr->vjt", v_tiles[:, 0], w_imag) + jnp.einsum("irjt,ivjr->vjt", v_tiles[:, 1], w_real)
    return jnp.stack([x_real.reshape(VP, NS), x_imag.reshape(VP, NS)])


def reference(focus_direct, u_factors, v_factors, tile_ranks, onset_rec, onset_src):
    plus = focus_direct
    minus = None
    for sweep in range(ITERS):
        reflected = lax.map(forward_one, (u_factors, v_factors, tile_ranks, plus))
        minus = window(reflected, onset_rec).astype(jnp.bfloat16)
        adjoint = lax.map(adjoint_one, (u_factors, v_factors, tile_ranks, minus))
        returned = window(adjoint, onset_src)
        plus = (focus_direct.astype(jnp.float32) + returned).astype(jnp.bfloat16)
    return plus, minus
```

```python
import cmath
import functools
import math

import jax
import jax.numpy as jnp
from jax import lax
from jax.experimental import pallas as pl
from jax.experimental.pallas import tpu as pltpu
from jax.sharding import PartitionSpec as P

TILE = 256
RANK = 32
NT = 256
FLO = 8
ITERS = 2
CHUNK = 16
LANES = 128


def make_tables(count):
    index = FLO + jnp.arange(count, dtype=jnp.int32)
    sample = jnp.arange(NT, dtype=jnp.int32)
    phase = (index[:, None] * sample[None, :] % NT).astype(jnp.float32) * (2.0 * math.pi / NT)
    cosine = jnp.cos(phase)
    sine = jnp.sin(phase)
    inverse = jnp.stack([cosine, -sine]) * (2.0 / NT)
    forward = jnp.stack([cosine, -sine])
    return (inverse, forward)


def window(spectrum, onset):
    inverse, forward = make_tables(spectrum.shape[0])
    signal = jnp.einsum("fcvm,cft->vmt", spectrum, inverse, precision=lax.Precision.HIGHEST)
    keep = jnp.arange(NT, dtype=jnp.int32)[None, None, :] < onset[:, :, None]
    signal = jnp.where(keep, signal, jnp.zeros_like(signal))
    return jnp.einsum("vmt,cft->fcvm", signal, forward, precision=lax.Precision.HIGHEST)


def coefficients(v_fac, mask, focus):
    points = focus.shape[1]
    row_tiles = v_fac.shape[0]
    col_tiles = v_fac.shape[-1] // TILE
    source = focus.reshape(2, points, col_tiles, TILE)
    v_tiles = v_fac.reshape(row_tiles, 2, RANK, col_tiles, TILE)
    form = "irjt,vjt->ivjr"
    z_real = jnp.einsum(
        form, v_tiles[:, 0], source[0], preferred_element_type=jnp.float32
    ) + jnp.einsum(form, v_tiles[:, 1], source[1], preferred_element_type=jnp.float32)
    z_imag = jnp.einsum(
        form, v_tiles[:, 0], source[1], preferred_element_type=jnp.float32
    ) - jnp.einsum(form, v_tiles[:, 1], source[0], preferred_element_type=jnp.float32)
    z_real = jnp.where(mask, z_real, 0.0).astype(jnp.bfloat16)
    z_imag = jnp.where(mask, z_imag, 0.0).astype(jnp.bfloat16)
    return jnp.stack([z_real, z_imag])


def expand_rows(u_fac, coeff):
    col_tiles = u_fac.shape[0]
    row_tiles = u_fac.shape[-1] // TILE
    points = coeff.shape[2]
    u_tiles = u_fac.reshape(col_tiles, 2, RANK, row_tiles, TILE)
    other = "jrit,ivjr->vit"
    y_real = jnp.einsum(
        other, u_tiles[:, 0], coeff[0], preferred_element_type=jnp.float32
    ) - jnp.einsum(other, u_tiles[:, 1], coeff[1], preferred_element_type=jnp.float32)
    y_imag = jnp.einsum(
        other, u_tiles[:, 0], coeff[1], preferred_element_type=jnp.float32
    ) + jnp.einsum(other, u_tiles[:, 1], coeff[0], preferred_element_type=jnp.float32)
    return jnp.stack([y_real.reshape(points, -1), y_imag.reshape(points, -1)])


def forward_local(u_fac, v_fac, mask, focus):
    return expand_rows(u_fac, coefficients(v_fac, mask, focus))


def adjoint_local(u_fac, v_fac, mask, focus):
    points = focus.shape[1]
    col_tiles = u_fac.shape[0]
    row_tiles = v_fac.shape[0]
    receiver = focus.reshape(2, points, row_tiles, TILE)
    v_tiles = v_fac.reshape(row_tiles, 2, RANK, col_tiles, TILE)
    u_tiles = u_fac.reshape(col_tiles, 2, RANK, row_tiles, TILE)
    form = "jrit,vit->ivjr"
    w_real = jnp.einsum(
        form, u_tiles[:, 0], receiver[0], preferred_element_type=jnp.float32
    ) + jnp.einsum(form, u_tiles[:, 1], receiver[1], preferred_element_type=jnp.float32)
    w_imag = jnp.einsum(
        form, u_tiles[:, 0], receiver[1], preferred_element_type=jnp.float32
    ) - jnp.einsum(form, u_tiles[:, 1], receiver[0], preferred_element_type=jnp.float32)
    w_real = jnp.where(mask, w_real, 0.0).astype(jnp.bfloat16)
    w_imag = jnp.where(mask, w_imag, 0.0).astype(jnp.bfloat16)
    other = "irjt,ivjr->vjt"
    x_real = jnp.einsum(
        other, v_tiles[:, 0], w_real, preferred_element_type=jnp.float32
    ) - jnp.einsum(other, v_tiles[:, 1], w_imag, preferred_element_type=jnp.float32)
    x_imag = jnp.einsum(
        other, v_tiles[:, 0], w_imag, preferred_element_type=jnp.float32
    ) + jnp.einsum(other, v_tiles[:, 1], w_real, preferred_element_type=jnp.float32)
    return jnp.stack([x_real.reshape(points, -1), x_imag.reshape(points, -1)])


def per_device(focus_direct, u_factors, v_factors, tile_ranks, onset_rec, onset_src):
    freq_count = lax.axis_size("freq")
    rank_index = jnp.arange(RANK, dtype=jnp.int32)
    masks = (rank_index[None, None, None, :] < tile_ranks[:, :, :, None])[:, :, None]
    rec_block = onset_rec.shape[1]
    rec_piece = rec_block // freq_count
    src_piece = onset_src.shape[1] // freq_count
    freq_place = lax.axis_index("freq")
    rec_onset = lax.dynamic_slice_in_dim(onset_rec, freq_place * rec_piece, rec_piece, 1)
    src_onset = lax.dynamic_slice_in_dim(onset_src, freq_place * src_piece, src_piece, 1)
    plus = focus_direct
    minus = None
    for sweep in range(ITERS):
        partial_terms = jax.vmap(forward_local)(u_factors, v_factors, masks, plus)
        summed = lax.psum_scatter(
            partial_terms.astype(jnp.bfloat16), "src", scatter_dimension=3, tiled=True
        ).astype(jnp.float32)
        traces = lax.all_to_all(
            summed.astype(jnp.bfloat16), "freq", split_axis=3, concat_axis=0, tiled=True
        ).astype(summed.dtype)
        windowed = window(traces, rec_onset).astype(jnp.bfloat16)
        minus = lax.all_to_all(windowed, "freq", split_axis=0, concat_axis=3, tiled=True)
        minus_all = lax.all_gather(minus, "src", axis=3, tiled=True)
        adjoint = jax.vmap(adjoint_local)(u_factors, v_factors, masks, minus_all)
        source_traces = lax.all_to_all(
            adjoint.astype(jnp.bfloat16), "freq", split_axis=3, concat_axis=0, tiled=True
        ).astype(adjoint.dtype)
        src_windowed = window(source_traces, src_onset)
        returned = lax.all_to_all(
            src_windowed.astype(jnp.bfloat16), "freq", split_axis=0, concat_axis=3, tiled=True
        ).astype(src_windowed.dtype)
        plus = (focus_direct.astype(jnp.float32) + returned).astype(jnp.bfloat16)
    return (plus, minus)


def lane_index(rows):
    return lax.broadcasted_iota(jnp.int32, (rows, LANES), 1)


def combine(x):
    half = x.shape[0] // 2
    lane = lane_index(x.shape[0])
    row = lax.broadcasted_iota(jnp.int32, x.shape, 0)
    first = (lane % (2 * RANK)) < RANK
    other = jnp.concatenate([x[half:], x[:half]], axis=0)
    moved = jnp.where(first, pltpu.roll(other, LANES - RANK, 1), pltpu.roll(other, RANK, 1))
    return jnp.where(first == (row < half), x + moved, x - moved)


def pair_up(a, b):
    low = lane_index(a.shape[0]) < 2 * RANK
    return (
        jnp.where(low, a, pltpu.roll(b, 2 * RANK, 1)),
        jnp.where(low, pltpu.roll(a, 2 * RANK, 1), b),
    )


def masked(x, rank_a, rank_b):
    lane = lane_index(x.shape[0])
    rank = jnp.where(lane < 2 * RANK, rank_a, rank_b)
    return jnp.where(lane % RANK < rank, x, 0.0).astype(jnp.bfloat16)


def times(a, b):
    return (a[0] * b[0] - a[1] * b[1], a[0] * b[1] + a[1] * b[0])


def window_terms(onset, count):
    samples = onset.astype(jnp.float32)
    angle = (samples - NT / 2) * (math.pi / NT)
    square = angle * angle

    def series(top):
        total = jnp.full_like(square, 1.0)
        for n in range(top, 1, -2):
            total = 1.0 - square * total * (1.0 / (n * (n - 1)))
        return total

    sin_half = angle * series(13)
    cos_half = series(14)
    z = (sin_half * sin_half - cos_half * cos_half, -2.0 * sin_half * cos_half)
    powers = {1: z}

    def power(m):
        if m not in powers:
            low = m // 2 if m % 2 == 0 else m - 1
            powers[m] = times(power(low), power(m - low))
        return powers[m]

    def term(m):
        if m == 0:
            return (samples * (1.0 / NT), None)
        scale = 1.0 / (cmath.exp(2j * math.pi * m / NT) - 1.0) / NT
        re, im = power(m)
        re = re - 1.0
        return (re * scale.real - im * scale.imag, re * scale.imag + im * scale.real)

    return [term(m) for m in range(count)], [term(m) for m in range(2 * FLO, 2 * (FLO + count) - 1)]


def window_block(spectra, onset, count):
    diff, total = window_terms(onset, count)
    results = []
    for out in range(count):
        real = imag = None
        for f in range(count):
            x_re, x_im = spectra[f]
            s_re, s_im = total[f + out]
            d_re, d_im = diff[abs(f - out)]
            if d_im is None:
                a, b, c, d = d_re + s_re, -s_im, -s_im, d_re - s_re
            else:
                if f < out:
                    d_im = -d_im
                a, b, c, d = d_re + s_re, -(d_im + s_im), d_im - s_im, d_re - s_re
            one, two = x_re * a + x_im * b, x_re * c + x_im * d
            real = one if real is None else real + one
            imag = two if imag is None else imag + two
        results.append((real, imag))
    return results


NT_DOT = (((1,), (1,)), ((), ()))


def kernel(
    axes, focus_hbm, u_hbm, v_hbm, ranks, onset_rec_hbm, onset_src_hbm, plus_hbm, minus_hbm,
    focus, u_fac, v_fac, onset_rec, onset_src, plus, coeff, back, kept,
    x_out, x_in, a_out, a_in, b_out, b_in, d_in, g_out, g_in, h_out, h_in,
    load_sem, store_sem, x_sems, d_sems, a_sems, b_sems, g_sems, h_sems,
):
    freqs, sides = axes["freq"], axes["src"]
    here = lax.axis_index("freq")
    side = lax.axis_index("src")
    partner = 1 - side
    points = focus.shape[1]
    chunks = points // CHUNK
    row_tiles = u_fac.shape[1] // TILE
    col_tiles = v_fac.shape[1] // TILE
    half = row_tiles // sides
    rec_piece = onset_rec.shape[1]
    src_piece = onset_src.shape[1]
    tiles_each = src_piece // TILE

    loads = [
        pltpu.make_async_copy(focus_hbm, focus, load_sem.at[0]),
        pltpu.make_async_copy(v_hbm, v_fac, load_sem.at[1]),
        pltpu.make_async_copy(u_hbm, u_fac, load_sem.at[2]),
        pltpu.make_async_copy(
            onset_rec_hbm.at[:, pl.ds(pl.multiple_of(here * rec_piece, LANES), rec_piece)], onset_rec, load_sem.at[3]
        ),
        pltpu.make_async_copy(
            onset_src_hbm.at[:, pl.ds(pl.multiple_of(here * src_piece, LANES), src_piece)], onset_src, load_sem.at[4]
        ),
    ]
    for load in loads:
        load.start()

    barrier = pltpu.get_barrier_semaphore()
    for step in range(1, freqs):
        pl.semaphore_signal(
            barrier, inc=1, device_id={"freq": lax.rem(here + step, freqs)}, device_id_type=pl.DeviceIdType.MESH
        )
    pl.semaphore_signal(barrier, inc=1, device_id={"src": partner}, device_id_type=pl.DeviceIdType.MESH)
    pl.semaphore_wait(barrier, freqs)

    sends = []
    stores = []

    def columns(index, size=TILE):
        return pl.ds(pl.multiple_of(index * size, size), size)

    def across(source, target, sems, k):
        return pltpu.make_async_remote_copy(
            src_ref=source, dst_ref=target, send_sem=sems.at[0, k], recv_sem=sems.at[1, k],
            device_id={"src": partner}, device_id_type=pl.DeviceIdType.MESH,
        )

    def along(out, into, sems, k, step):
        target = lax.rem(here + step, freqs)
        return pltpu.make_async_remote_copy(
            src_ref=out.at[k, target], dst_ref=into.at[k, here],
            send_sem=sems.at[0, k, step - 1], recv_sem=sems.at[1, k, step - 1],
            device_id={"freq": target}, device_id_type=pl.DeviceIdType.MESH,
        )

    def arrived(out, into, sems, k, step):
        source = lax.rem(here + freqs - step, freqs)
        pltpu.make_async_remote_copy(
            src_ref=out.at[k, source], dst_ref=into.at[k, source],
            send_sem=sems.at[0, k, step - 1], recv_sem=sems.at[1, k, step - 1],
            device_id={"freq": source}, device_id_type=pl.DeviceIdType.MESH,
        ).wait_recv()

    def send(copy):
        copy.start()
        sends.append(copy)

    def spread_out(first, second, into, store):
        for q in range(first.shape[1] // LANES):
            lanes = slice(q * LANES, (q + 1) * LANES)
            even, odd = pair_up(combine(first[:, lanes]), combine(second[:, lanes]))
            store(2 * q, even)
            store(2 * q + 1, odd)

    def forward(sweep, c):
        k = sweep * chunks + c
        rows = slice(c * CHUNK, (c + 1) * CHUNK)

        def one(pair, carry):
            products = []
            for t in range(2):
                cols = columns(2 * pair + t)
                if sweep == 0:
                    block = focus[:, rows, cols].reshape(2 * CHUNK, TILE)
                else:
                    block = plus[c, :, cols]
                products.append(lax.dot_general(block, v_fac[:, cols], NT_DOT, preferred_element_type=jnp.float32))

            def store(i, value):
                coeff[i, :, columns(pair, LANES)] = masked(value, ranks[i, 2 * pair], ranks[i, 2 * pair + 1])

            spread_out(products[0], products[1], coeff, store)
            return carry

        lax.fori_loop(0, col_tiles // 2, one, 0)
        if sweep == 0 and c == 0:
            loads[2].wait()

        def product(i):
            return jnp.dot(coeff[i], u_fac[:, columns(i)], preferred_element_type=jnp.float32)

        def theirs(n, carry):
            x_out[k, :, columns(n)] = product(partner * half + n).astype(jnp.bfloat16)
            return carry

        def ours(n, carry):
            kept[c, :, columns(n)] = product(side * half + n)
            return carry

        lax.fori_loop(0, half, theirs, 0)
        send(across(x_out.at[k], x_in.at[k], x_sems, k))
        lax.fori_loop(0, half, ours, 0)

    def reduce(sweep, c):
        k = sweep * chunks + c
        across(x_out.at[k], x_in.at[k], x_sems, k).wait_recv()
        for q in range(freqs):
            lanes = slice(q * rec_piece, (q + 1) * rec_piece)
            a_out[k, q] = (kept[c, :, lanes] + x_in[k, :, lanes].astype(jnp.float32)).astype(jnp.bfloat16)
        for step in range(1, freqs):
            send(along(a_out, a_in, a_sems, k, step))
        a_in[k, here] = a_out[k, here]

    def window(k, c, from_ref, to_ref, own_ref, onset):
        rows = slice(c * CHUNK, (c + 1) * CHUNK)

        def one(n, carry):
            lanes = columns(n, LANES)
            spectra = []
            for f in range(freqs):
                both = from_ref[k, f, :, lanes].astype(jnp.float32)
                spectra.append((both[:CHUNK], both[CHUNK:]))
            for f, (real, imag) in enumerate(window_block(spectra, onset[rows, lanes], freqs)):
                to_ref[k, f, :, lanes] = jnp.concatenate([real, imag], axis=0).astype(jnp.bfloat16)
            return carry

        lax.fori_loop(0, onset.shape[1] // LANES, one, 0)

    def window_rec(sweep, c):
        k = sweep * chunks + c
        if sweep == 0 and c == 0:
            loads[3].wait()
        for step in range(1, freqs):
            arrived(a_out, a_in, a_sems, k, step)
        window(k, c, a_in, b_out, b_in, onset_rec)
        for step in range(1, freqs):
            send(along(b_out, b_in, b_sems, k, step))
        b_in[k, here] = b_out[k, here]

    def spread(sweep, c):
        k = sweep * chunks + c
        for step in range(1, freqs):
            arrived(b_out, b_in, b_sems, k, step)
        send(across(b_in.at[k], d_in.at[k], d_sems, k))
        if sweep == ITERS - 1:
            for part in range(2):
                for q in range(freqs):
                    store = pltpu.make_async_copy(
                        b_in.at[k, q, pl.ds(part * CHUNK, CHUNK), :],
                        minus_hbm.at[part, pl.ds(c * CHUNK, CHUNK), pl.ds(q * rec_piece, rec_piece)],
                        store_sem.at[1, c, part * freqs + q],
                    )
                    store.start()
                    stores.append(store)

    def adjoint(sweep, c):
        k = sweep * chunks + c

        def back_pairs(source, first_tile):
            def one(pair, carry):
                products = []
                for t in range(2):
                    n = 2 * pair + t
                    block = source[k, n * TILE // rec_piece, :, pl.ds(pl.multiple_of(n * TILE % rec_piece, LANES), TILE)]
                    products.append(
                        lax.dot_general(
                            block, u_fac[:, columns(first_tile + n)], NT_DOT, preferred_element_type=jnp.float32
                        )
                    )
                at = first_tile // 2 + pair

                def store(j, value):
                    back[j, :, columns(at, LANES)] = masked(value, ranks[2 * at, j], ranks[2 * at + 1, j])

                spread_out(products[0], products[1], back, store)
                return carry

            lax.fori_loop(0, half // 2, one, 0)

        back_pairs(b_in, side * half)
        across(b_in.at[k], d_in.at[k], d_sems, k).wait_recv()
        back_pairs(d_in, partner * half)

        for step in list(range(1, freqs)) + [0]:
            target = lax.rem(here + step, freqs)

            def one(n, carry):
                j = target * tiles_each + n
                value = jnp.dot(back[j], v_fac[:, columns(j)], preferred_element_type=jnp.float32).astype(jnp.bfloat16)
                if step == 0:
                    g_in[k, here, :, columns(n)] = value
                else:
                    g_out[k, target, :, columns(n)] = value
                return carry

            lax.fori_loop(0, tiles_each, one, 0)
            if step > 0:
                send(along(g_out, g_in, g_sems, k, step))

    def window_src(sweep, c):
        k = sweep * chunks + c
        if sweep == 0 and c == 0:
            loads[4].wait()
        for step in range(1, freqs):
            arrived(g_out, g_in, g_sems, k, step)
        window(k, c, g_in, h_out, h_in, onset_src)
        for step in range(1, freqs):
            send(along(h_out, h_in, h_sems, k, step))
        h_in[k, here] = h_out[k, here]

    def finish(sweep, c):
        k = sweep * chunks + c
        rows = slice(c * CHUNK, (c + 1) * CHUNK)
        for step in range(1, freqs):
            arrived(h_out, h_in, h_sems, k, step)
        last = sweep == ITERS - 1
        base = chunks if last else 0
        for q in range(freqs):
            lanes = slice(q * src_piece, (q + 1) * src_piece)
            start = focus[:, rows, lanes].reshape(2 * CHUNK, src_piece).astype(jnp.float32)
            plus[base + c, :, lanes] = (start + h_in[k, q].astype(jnp.float32)).astype(jnp.bfloat16)
        if last:
            for part in range(2):
                store = pltpu.make_async_copy(
                    plus.at[base + c, pl.ds(part * CHUNK, CHUNK), :],
                    plus_hbm.at[part, pl.ds(c * CHUNK, CHUNK), :],
                    store_sem.at[0, c, part],
                )
                store.start()
                stores.append(store)

    loads[0].wait()
    loads[1].wait()
    stages = [forward, reduce, window_rec, spread, adjoint, window_src, finish]
    for sweep in range(ITERS):
        for stage in stages:
            for c in range(chunks):
                stage(sweep, c)
    for copy in sends:
        copy.wait_send()
    for store in stores:
        store.wait()


def whole_in_one(axes, focus_direct, u_factors, v_factors, tile_ranks, onset_rec, onset_src):
    freqs = axes["freq"]
    points, sources = focus_direct.shape[2:]
    receivers = u_factors.shape[-1]
    block = onset_rec.shape[1]
    rec_piece, src_piece = block // freqs, sources // freqs
    row_tiles, col_tiles = receivers // TILE, sources // TILE
    chunks = points // CHUNK
    runs = ITERS * chunks
    rows = 2 * CHUNK
    bf16, f32 = jnp.bfloat16, jnp.float32
    small = pltpu.VMEM((runs, freqs, rows, rec_piece), bf16)
    large = pltpu.VMEM((runs, freqs, rows, src_piece), bf16)
    dma = pltpu.SemaphoreType.DMA
    anywhere = pl.BlockSpec(memory_space=pl.ANY)
    plus, minus = pl.pallas_call(
        functools.partial(kernel, axes),
        out_shape=(
            jax.ShapeDtypeStruct((2, points, sources), bf16),
            jax.ShapeDtypeStruct((2, points, block), bf16),
        ),
        in_specs=[anywhere, anywhere, anywhere, pl.BlockSpec(memory_space=pltpu.SMEM), anywhere, anywhere],
        out_specs=(anywhere, anywhere),
        scratch_shapes=[
            pltpu.VMEM((2, points, sources), bf16),
            pltpu.VMEM((col_tiles * 2 * RANK, receivers), bf16),
            pltpu.VMEM((row_tiles * 2 * RANK, sources), bf16),
            pltpu.VMEM((points, rec_piece), jnp.int32),
            pltpu.VMEM((points, src_piece), jnp.int32),
            pltpu.VMEM((2 * chunks, rows, sources), bf16),
            pltpu.VMEM((row_tiles, rows, col_tiles * 2 * RANK), bf16),
            pltpu.VMEM((col_tiles, rows, row_tiles * 2 * RANK), bf16),
            pltpu.VMEM((chunks, rows, block), f32),
            pltpu.VMEM((runs, rows, block), bf16),
            pltpu.VMEM((runs, rows, block), bf16),
            small, small, small, small, small,
            large, large, large, large,
            dma((5,)),
            dma((2, chunks, 2 * freqs)),
            dma((2, runs)),
            dma((2, runs)),
            dma((2, runs, freqs - 1)),
            dma((2, runs, freqs - 1)),
            dma((2, runs, freqs - 1)),
            dma((2, runs, freqs - 1)),
        ],
        compiler_params=pltpu.CompilerParams(
            collective_id=0, has_side_effects=True, vmem_limit_bytes=48 * 1024 * 1024
        ),
    )(
        focus_direct[0],
        u_factors.reshape(col_tiles * 2 * RANK, receivers),
        v_factors.reshape(row_tiles * 2 * RANK, sources),
        tile_ranks[0],
        onset_rec,
        onset_src,
    )
    return plus[None], minus[None]


def fits(axes, focus_direct, u_factors, onset_rec):
    freqs, sides = axes["freq"], axes["src"]
    points, sources = focus_direct.shape[2:]
    receivers = u_factors.shape[-1]
    return (
        sides == 2
        and focus_direct.shape[0] == 1
        and freqs > 1
        and points % CHUNK == 0
        and onset_rec.shape[1] % (freqs * TILE) == 0
        and sources % (freqs * TILE) == 0
        and receivers % (sides * 2 * TILE) == 0
    )


def solution(mesh):
    placed = (
        P("freq", None, ("groups", "vp"), "src"),
        P("freq", "src", None, None, None),
        P("freq", None, None, None, "src"),
        P("freq", None, "src"),
        P(("groups", "vp"), "src"),
        P(("groups", "vp"), "src"),
    )
    axes = dict(mesh.shape)

    def part(focus_direct, u_factors, v_factors, tile_ranks, onset_rec, onset_src):
        args = (focus_direct, u_factors, v_factors, tile_ranks, onset_rec, onset_src)
        if fits(axes, focus_direct, u_factors, onset_rec):
            return whole_in_one(axes, *args)
        return per_device(*args)

    return jax.shard_map(
        part,
        mesh=mesh,
        in_specs=placed,
        out_specs=(
            P("freq", None, ("groups", "vp"), "src"),
            P("freq", None, ("groups", "vp"), "src"),
        ),
        check_vma=False,
    )
```

```python
import cmath
import functools
import math

import jax
import jax.numpy as jnp
from jax import lax
from jax.experimental import pallas as pl
from jax.experimental.pallas import tpu as pltpu
from jax.sharding import PartitionSpec as P

TILE = 256
RANK = 32
NT = 256
FLO = 8
ITERS = 2
CHUNK = 16
LANES = 128
VMEM_BYTES = 64 * 1024 * 1024 - 512 * 1024


ORDER = (
    0, 1, 100, 2, 101, 200, 102, 300, 201, 202, 400, 301, 401, 500,
    302, 402, 501, 600, 10, 502, 601, 11, 110, 111, 602, 12, 211, 112,
    311, 210, 212, 411, 312, 310, 412, 410, 511, 512, 510, 611, 612, 610,
)


def make_tables(count):
    index = FLO + jnp.arange(count, dtype=jnp.int32)
    sample = jnp.arange(NT, dtype=jnp.int32)
    phase = (index[:, None] * sample[None, :] % NT).astype(jnp.float32) * (2.0 * math.pi / NT)
    cosine = jnp.cos(phase)
    sine = jnp.sin(phase)
    inverse = jnp.stack([cosine, -sine]) * (2.0 / NT)
    forward = jnp.stack([cosine, -sine])
    return (inverse, forward)


def window(spectrum, onset):
    inverse, forward = make_tables(spectrum.shape[0])
    signal = jnp.einsum("fcvm,cft->vmt", spectrum, inverse, precision=lax.Precision.HIGHEST)
    keep = jnp.arange(NT, dtype=jnp.int32)[None, None, :] < onset[:, :, None]
    signal = jnp.where(keep, signal, jnp.zeros_like(signal))
    return jnp.einsum("vmt,cft->fcvm", signal, forward, precision=lax.Precision.HIGHEST)


def coefficients(v_fac, mask, focus):
    points = focus.shape[1]
    row_tiles = v_fac.shape[0]
    col_tiles = v_fac.shape[-1] // TILE
    source = focus.reshape(2, points, col_tiles, TILE)
    v_tiles = v_fac.reshape(row_tiles, 2, RANK, col_tiles, TILE)
    form = "irjt,vjt->ivjr"
    z_real = jnp.einsum(
        form, v_tiles[:, 0], source[0], preferred_element_type=jnp.float32
    ) + jnp.einsum(form, v_tiles[:, 1], source[1], preferred_element_type=jnp.float32)
    z_imag = jnp.einsum(
        form, v_tiles[:, 0], source[1], preferred_element_type=jnp.float32
    ) - jnp.einsum(form, v_tiles[:, 1], source[0], preferred_element_type=jnp.float32)
    z_real = jnp.where(mask, z_real, 0.0).astype(jnp.bfloat16)
    z_imag = jnp.where(mask, z_imag, 0.0).astype(jnp.bfloat16)
    return jnp.stack([z_real, z_imag])


def expand_rows(u_fac, coeff):
    col_tiles = u_fac.shape[0]
    row_tiles = u_fac.shape[-1] // TILE
    points = coeff.shape[2]
    u_tiles = u_fac.reshape(col_tiles, 2, RANK, row_tiles, TILE)
    other = "jrit,ivjr->vit"
    y_real = jnp.einsum(
        other, u_tiles[:, 0], coeff[0], preferred_element_type=jnp.float32
    ) - jnp.einsum(other, u_tiles[:, 1], coeff[1], preferred_element_type=jnp.float32)
    y_imag = jnp.einsum(
        other, u_tiles[:, 0], coeff[1], preferred_element_type=jnp.float32
    ) + jnp.einsum(other, u_tiles[:, 1], coeff[0], preferred_element_type=jnp.float32)
    return jnp.stack([y_real.reshape(points, -1), y_imag.reshape(points, -1)])


def forward_local(u_fac, v_fac, mask, focus):
    return expand_rows(u_fac, coefficients(v_fac, mask, focus))


def adjoint_local(u_fac, v_fac, mask, focus):
    points = focus.shape[1]
    col_tiles = u_fac.shape[0]
    row_tiles = v_fac.shape[0]
    receiver = focus.reshape(2, points, row_tiles, TILE)
    v_tiles = v_fac.reshape(row_tiles, 2, RANK, col_tiles, TILE)
    u_tiles = u_fac.reshape(col_tiles, 2, RANK, row_tiles, TILE)
    form = "jrit,vit->ivjr"
    w_real = jnp.einsum(
        form, u_tiles[:, 0], receiver[0], preferred_element_type=jnp.float32
    ) + jnp.einsum(form, u_tiles[:, 1], receiver[1], preferred_element_type=jnp.float32)
    w_imag = jnp.einsum(
        form, u_tiles[:, 0], receiver[1], preferred_element_type=jnp.float32
    ) - jnp.einsum(form, u_tiles[:, 1], receiver[0], preferred_element_type=jnp.float32)
    w_real = jnp.where(mask, w_real, 0.0).astype(jnp.bfloat16)
    w_imag = jnp.where(mask, w_imag, 0.0).astype(jnp.bfloat16)
    other = "irjt,ivjr->vjt"
    x_real = jnp.einsum(
        other, v_tiles[:, 0], w_real, preferred_element_type=jnp.float32
    ) - jnp.einsum(other, v_tiles[:, 1], w_imag, preferred_element_type=jnp.float32)
    x_imag = jnp.einsum(
        other, v_tiles[:, 0], w_imag, preferred_element_type=jnp.float32
    ) + jnp.einsum(other, v_tiles[:, 1], w_real, preferred_element_type=jnp.float32)
    return jnp.stack([x_real.reshape(points, -1), x_imag.reshape(points, -1)])


def per_device(focus_direct, u_factors, v_factors, tile_ranks, onset_rec, onset_src):
    freq_count = lax.axis_size("freq")
    rank_index = jnp.arange(RANK, dtype=jnp.int32)
    masks = (rank_index[None, None, None, :] < tile_ranks[:, :, :, None])[:, :, None]
    rec_block = onset_rec.shape[1]
    rec_piece = rec_block // freq_count
    src_piece = onset_src.shape[1] // freq_count
    freq_place = lax.axis_index("freq")
    rec_onset = lax.dynamic_slice_in_dim(onset_rec, freq_place * rec_piece, rec_piece, 1)
    src_onset = lax.dynamic_slice_in_dim(onset_src, freq_place * src_piece, src_piece, 1)
    plus = focus_direct
    minus = None
    for sweep in range(ITERS):
        partial_terms = jax.vmap(forward_local)(u_factors, v_factors, masks, plus)
        summed = lax.psum_scatter(
            partial_terms.astype(jnp.bfloat16), "src", scatter_dimension=3, tiled=True
        ).astype(jnp.float32)
        traces = lax.all_to_all(
            summed.astype(jnp.bfloat16), "freq", split_axis=3, concat_axis=0, tiled=True
        ).astype(summed.dtype)
        windowed = window(traces, rec_onset).astype(jnp.bfloat16)
        minus = lax.all_to_all(windowed, "freq", split_axis=0, concat_axis=3, tiled=True)
        minus_all = lax.all_gather(minus, "src", axis=3, tiled=True)
        adjoint = jax.vmap(adjoint_local)(u_factors, v_factors, masks, minus_all)
        source_traces = lax.all_to_all(
            adjoint.astype(jnp.bfloat16), "freq", split_axis=3, concat_axis=0, tiled=True
        ).astype(adjoint.dtype)
        src_windowed = window(source_traces, src_onset)
        returned = lax.all_to_all(
            src_windowed.astype(jnp.bfloat16), "freq", split_axis=0, concat_axis=3, tiled=True
        ).astype(src_windowed.dtype)
        plus = (focus_direct.astype(jnp.float32) + returned).astype(jnp.bfloat16)
    return (plus, minus)


def repeat(count, width, step):
    width = math.gcd(count, width)
    if count == width:
        for n in range(count):
            step(n)
        return

    def turn(n, carry):
        for t in range(width):
            step(n * width + t)
        return carry

    lax.fori_loop(0, count // width, turn, 0)


def lane_index(rows):
    return lax.broadcasted_iota(jnp.int32, (rows, LANES), 1)


def combine(x):
    half = x.shape[0] // 2
    lane = lane_index(x.shape[0])
    row = lax.broadcasted_iota(jnp.int32, x.shape, 0)
    first = (lane % (2 * RANK)) < RANK
    other = jnp.concatenate([x[half:], x[:half]], axis=0)
    moved = jnp.where(first, pltpu.roll(other, LANES - RANK, 1), pltpu.roll(other, RANK, 1))
    return jnp.where(first == (row < half), x + moved, x - moved)


def pair_up(a, b):
    low = lane_index(a.shape[0]) < 2 * RANK
    return (
        jnp.where(low, a, pltpu.roll(b, 2 * RANK, 1)),
        jnp.where(low, pltpu.roll(a, 2 * RANK, 1), b),
    )


def masked(x, rank_a, rank_b):
    lane = lane_index(x.shape[0])
    rank = jnp.where(lane < 2 * RANK, rank_a, rank_b)
    return jnp.where(lane % RANK < rank, x, 0.0).astype(jnp.bfloat16)


def times(a, b):
    return (a[0] * b[0] - a[1] * b[1], a[0] * b[1] + a[1] * b[0])


def window_terms(onset, count):
    samples = onset.astype(jnp.float32)
    angle = (samples - NT / 2) * (math.pi / NT)
    square = angle * angle

    def series(top):
        total = jnp.full_like(square, 1.0)
        for n in range(top, 1, -2):
            total = 1.0 - square * total * (1.0 / (n * (n - 1)))
        return total

    sin_half = angle * series(13)
    cos_half = series(14)
    z = (sin_half * sin_half - cos_half * cos_half, -2.0 * sin_half * cos_half)
    powers = {1: z}

    def power(m):
        if m not in powers:
            low = m // 2 if m % 2 == 0 else m - 1
            powers[m] = times(power(low), power(m - low))
        return powers[m]

    def term(m):
        if m == 0:
            return (samples * (1.0 / NT), None)
        scale = 1.0 / (cmath.exp(2j * math.pi * m / NT) - 1.0) / NT
        re, im = power(m)
        re = re - 1.0
        return (re * scale.real - im * scale.imag, re * scale.imag + im * scale.real)

    return [term(m) for m in range(count)], [term(m) for m in range(2 * FLO, 2 * (FLO + count) - 1)]


def window_block(spectra, onset, count):
    diff, total = window_terms(onset, count)
    results = []
    for out in range(count):
        real = imag = None
        for f in range(count):
            x_re, x_im = spectra[f]
            s_re, s_im = total[f + out]
            d_re, d_im = diff[abs(f - out)]
            if d_im is None:
                a, b, c, d = d_re + s_re, -s_im, -s_im, d_re - s_re
            else:
                if f < out:
                    d_im = -d_im
                a, b, c, d = d_re + s_re, -(d_im + s_im), d_im - s_im, d_re - s_re
            one, two = x_re * a + x_im * b, x_re * c + x_im * d
            real = one if real is None else real + one
            imag = two if imag is None else imag + two
        results.append((real, imag))
    return results


NT_DOT = (((1,), (1,)), ((), ()))


def kernel(
    axes, focus_hbm, u_hbm, v_hbm, ranks_hbm, onset_rec_hbm, onset_src_hbm, plus_hbm, minus_hbm,
    ranks, focus, u_fac, v_fac, onset_rec, onset_src, plus, coeff, back, kept,
    x_out, x_in, a_out, a_in, b_out, b_in, d_in, g_out, g_in, h_out, h_in,
    load_sem, store_sem, x_sems, d_sems, a_sems, b_sems, g_sems, h_sems,
):
    freqs, sides = axes["freq"], axes["src"]
    here = lax.axis_index("freq")
    side = lax.axis_index("src")
    partner = 1 - side
    points = focus.shape[1]
    chunks = points // CHUNK
    row_tiles = u_fac.shape[1] // TILE
    col_tiles = v_fac.shape[1] // TILE
    half = row_tiles // sides
    rec_piece = onset_rec.shape[1]
    src_piece = onset_src.shape[1]
    tiles_each = src_piece // TILE

    loads = [
        pltpu.make_async_copy(focus_hbm, focus, load_sem.at[0]),
        pltpu.make_async_copy(ranks_hbm, ranks, load_sem.at[5]),
        pltpu.make_async_copy(v_hbm, v_fac, load_sem.at[1]),
        pltpu.make_async_copy(u_hbm, u_fac, load_sem.at[2]),
        pltpu.make_async_copy(
            onset_rec_hbm.at[:, pl.ds(pl.multiple_of(here * rec_piece, LANES), rec_piece)], onset_rec, load_sem.at[3]
        ),
        pltpu.make_async_copy(
            onset_src_hbm.at[:, pl.ds(pl.multiple_of(here * src_piece, LANES), src_piece)], onset_src, load_sem.at[4]
        ),
    ]
    for load in loads:
        load.start()

    barrier = pltpu.get_barrier_semaphore()
    for step in range(1, freqs):
        pl.semaphore_signal(
            barrier, inc=1, device_id={"freq": lax.rem(here + step, freqs)}, device_id_type=pl.DeviceIdType.MESH
        )
    pl.semaphore_signal(barrier, inc=1, device_id={"src": partner}, device_id_type=pl.DeviceIdType.MESH)

    sends = []
    stores = []

    def columns(index, size=TILE):
        if isinstance(index, int):
            return pl.ds(index * size, size)
        return pl.ds(pl.multiple_of(index * size, size), size)

    def across(source, target, sems, k):
        return pltpu.make_async_remote_copy(
            src_ref=source, dst_ref=target, send_sem=sems.at[0, k], recv_sem=sems.at[1, k],
            device_id={"src": partner}, device_id_type=pl.DeviceIdType.MESH,
        )

    def along(out, into, sems, k, step):
        target = lax.rem(here + step, freqs)
        return pltpu.make_async_remote_copy(
            src_ref=out.at[k, target], dst_ref=into.at[k, here],
            send_sem=sems.at[0, k, step - 1], recv_sem=sems.at[1, k, step - 1],
            device_id={"freq": target}, device_id_type=pl.DeviceIdType.MESH,
        )

    def arrived(out, into, sems, k, step):
        source = lax.rem(here + freqs - step, freqs)
        pltpu.make_async_remote_copy(
            src_ref=out.at[k, source], dst_ref=into.at[k, source],
            send_sem=sems.at[0, k, step - 1], recv_sem=sems.at[1, k, step - 1],
            device_id={"freq": source}, device_id_type=pl.DeviceIdType.MESH,
        ).wait_recv()

    def send(copy):
        copy.start()
        sends.append(copy)

    def spread_out(first, second, store):
        for q in range(first.shape[1] // LANES):
            lanes = slice(q * LANES, (q + 1) * LANES)
            even, odd = pair_up(combine(first[:, lanes]), combine(second[:, lanes]))
            store(2 * q, even)
            store(2 * q + 1, odd)

    def forward(sweep, c):
        k = sweep * chunks + c
        rows = slice(c * CHUNK, (c + 1) * CHUNK)

        def one(pair):
            products = []
            for t in range(2):
                cols = columns(2 * pair + t)
                if sweep == 0:
                    block = focus[:, rows, cols].reshape(2 * CHUNK, TILE)
                else:
                    block = plus[c, :, cols]
                products.append(lax.dot_general(block, v_fac[:, cols], NT_DOT, preferred_element_type=jnp.float32))

            def store(i, value):
                coeff[i, :, columns(pair, LANES)] = masked(value, ranks[i, 2 * pair], ranks[i, 2 * pair + 1])

            spread_out(products[0], products[1], store)

        repeat(col_tiles // 2, 2, one)
        if sweep == 0 and c == 0:
            loads[3].wait()

        def product(i):
            return jnp.dot(coeff[i], u_fac[:, columns(i)], preferred_element_type=jnp.float32)

        def theirs(n):
            x_out[k, :, columns(n)] = product(partner * half + n).astype(jnp.bfloat16)

        def ours(n):
            kept[c, :, columns(n)] = product(side * half + n)

        for n in range(half):
            theirs(n)
        if sweep == 0 and c == 0:
            pl.semaphore_wait(barrier, freqs)
        send(across(x_out.at[k], x_in.at[k], x_sems, k))
        for n in range(half):
            ours(n)

    def reduce(sweep, c):
        k = sweep * chunks + c
        across(x_out.at[k], x_in.at[k], x_sems, k).wait_recv()
        for q in range(freqs):
            lanes = slice(q * rec_piece, (q + 1) * rec_piece)
            a_out[k, q] = (kept[c, :, lanes] + x_in[k, :, lanes].astype(jnp.float32)).astype(jnp.bfloat16)
        for step in range(1, freqs):
            send(along(a_out, a_in, a_sems, k, step))
        a_in[k, here] = a_out[k, here]

    def window(k, c, from_ref, to_ref, own_ref, onset):
        rows = slice(c * CHUNK, (c + 1) * CHUNK)

        def one(n):
            lanes = columns(n, LANES)
            spectra = []
            for f in range(freqs):
                both = from_ref[k, f, :, lanes].astype(jnp.float32)
                spectra.append((both[:CHUNK], both[CHUNK:]))
            for f, (real, imag) in enumerate(window_block(spectra, onset[rows, lanes], freqs)):
                to_ref[k, f, :, lanes] = jnp.concatenate([real, imag], axis=0).astype(jnp.bfloat16)

        repeat(onset.shape[1] // LANES, 2, one)

    def window_rec(sweep, c):
        k = sweep * chunks + c
        if sweep == 0 and c == 0:
            loads[4].wait()
        for step in range(1, freqs):
            arrived(a_out, a_in, a_sems, k, step)
        window(k, c, a_in, b_out, b_in, onset_rec)
        for step in range(1, freqs):
            send(along(b_out, b_in, b_sems, k, step))
        b_in[k, here] = b_out[k, here]

    def spread(sweep, c):
        k = sweep * chunks + c
        for step in range(1, freqs):
            arrived(b_out, b_in, b_sems, k, step)
        send(across(b_in.at[k], d_in.at[k], d_sems, k))
        if sweep == ITERS - 1:
            for part in range(2):
                for q in range(freqs):
                    store = pltpu.make_async_copy(
                        b_in.at[k, q, pl.ds(part * CHUNK, CHUNK), :],
                        minus_hbm.at[part, pl.ds(c * CHUNK, CHUNK), pl.ds(q * rec_piece, rec_piece)],
                        store_sem.at[1, c, part * freqs + q],
                    )
                    store.start()
                    stores.append(store)

    def adjoint(sweep, c):
        k = sweep * chunks + c

        def back_pairs(source, first_tile):
            def one(pair):
                products = []
                for t in range(2):
                    n = 2 * pair + t
                    block = source[k, n * TILE // rec_piece, :, pl.ds(pl.multiple_of(n * TILE % rec_piece, LANES), TILE)]
                    products.append(
                        lax.dot_general(
                            block, u_fac[:, columns(first_tile + n)], NT_DOT, preferred_element_type=jnp.float32
                        )
                    )
                at = first_tile // 2 + pair

                def store(j, value):
                    back[j, :, columns(at, LANES)] = masked(value, ranks[2 * at, j], ranks[2 * at + 1, j])

                spread_out(products[0], products[1], store)

            repeat(half // 2, 2, one)

        back_pairs(b_in, side * half)
        across(b_in.at[k], d_in.at[k], d_sems, k).wait_recv()
        back_pairs(d_in, partner * half)

        for step in list(range(1, freqs)) + [0]:
            target = lax.rem(here + step, freqs)

            def one(n):
                j = target * tiles_each + n
                value = jnp.dot(back[j], v_fac[:, columns(j)], preferred_element_type=jnp.float32).astype(jnp.bfloat16)
                if step == 0:
                    g_in[k, here, :, columns(n)] = value
                else:
                    g_out[k, target, :, columns(n)] = value

            repeat(tiles_each, 4, one)
            if step > 0:
                send(along(g_out, g_in, g_sems, k, step))

    def window_src(sweep, c):
        k = sweep * chunks + c
        if sweep == 0 and c == 0:
            loads[5].wait()
        for step in range(1, freqs):
            arrived(g_out, g_in, g_sems, k, step)
        window(k, c, g_in, h_out, h_in, onset_src)
        for step in range(1, freqs):
            send(along(h_out, h_in, h_sems, k, step))
        h_in[k, here] = h_out[k, here]

    def finish(sweep, c):
        k = sweep * chunks + c
        rows = slice(c * CHUNK, (c + 1) * CHUNK)
        for step in range(1, freqs):
            arrived(h_out, h_in, h_sems, k, step)
        last = sweep == ITERS - 1
        base = chunks if last else 0
        for q in range(freqs):
            lanes = slice(q * src_piece, (q + 1) * src_piece)
            start = focus[:, rows, lanes].reshape(2 * CHUNK, src_piece).astype(jnp.float32)
            plus[base + c, :, lanes] = (start + h_in[k, q].astype(jnp.float32)).astype(jnp.bfloat16)
        if last:
            for part in range(2):
                store = pltpu.make_async_copy(
                    plus.at[base + c, pl.ds(part * CHUNK, CHUNK), :],
                    plus_hbm.at[part, pl.ds(c * CHUNK, CHUNK), :],
                    store_sem.at[0, c, part],
                )
                store.start()
                stores.append(store)

    for load in loads[:3]:
        load.wait()
    stages = [forward, reduce, window_rec, spread, adjoint, window_src, finish]
    for stage, sweep, c in order_of(chunks):
        stages[stage](sweep, c)
    for copy in sends:
        copy.wait_send()
    for store in stores:
        store.wait()


def order_of(chunks):
    if chunks == 3:
        return [(code // 100, code // 10 % 10, code % 10) for code in ORDER]
    return [(stage, sweep, c) for sweep in range(ITERS) for stage in range(7) for c in range(chunks)]


def whole_in_one(axes, focus_direct, u_factors, v_factors, tile_ranks, onset_rec, onset_src):
    freqs = axes["freq"]
    points, sources = focus_direct.shape[2:]
    receivers = u_factors.shape[-1]
    block = onset_rec.shape[1]
    rec_piece, src_piece = block // freqs, sources // freqs
    row_tiles, col_tiles = receivers // TILE, sources // TILE
    chunks = points // CHUNK
    runs = ITERS * chunks
    rows = 2 * CHUNK
    bf16, f32 = jnp.bfloat16, jnp.float32
    small = pltpu.VMEM((runs, freqs, rows, rec_piece), bf16)
    large = pltpu.VMEM((runs, freqs, rows, src_piece), bf16)
    dma = pltpu.SemaphoreType.DMA
    anywhere = pl.BlockSpec(memory_space=pl.ANY)
    plus, minus = pl.pallas_call(
        functools.partial(kernel, axes),
        out_shape=(
            jax.ShapeDtypeStruct((2, points, sources), bf16),
            jax.ShapeDtypeStruct((2, points, block), bf16),
        ),
        in_specs=[anywhere] * 6,
        out_specs=(anywhere, anywhere),
        scratch_shapes=[
            pltpu.SMEM((row_tiles, col_tiles), jnp.int32),
            pltpu.VMEM((2, points, sources), bf16),
            pltpu.VMEM((col_tiles * 2 * RANK, receivers), bf16),
            pltpu.VMEM((row_tiles * 2 * RANK, sources), bf16),
            pltpu.VMEM((points, rec_piece), jnp.int32),
            pltpu.VMEM((points, src_piece), jnp.int32),
            pltpu.VMEM((2 * chunks, rows, sources), bf16),
            pltpu.VMEM((row_tiles, rows, col_tiles * 2 * RANK), bf16),
            pltpu.VMEM((col_tiles, rows, row_tiles * 2 * RANK), bf16),
            pltpu.VMEM((chunks, rows, block), f32),
            pltpu.VMEM((runs, rows, block), bf16),
            pltpu.VMEM((runs, rows, block), bf16),
            small, small, small, small, small,
            large, large, large, large,
            dma((6,)),
            dma((2, chunks, 2 * freqs)),
            dma((2, runs)),
            dma((2, runs)),
            dma((2, runs, freqs - 1)),
            dma((2, runs, freqs - 1)),
            dma((2, runs, freqs - 1)),
            dma((2, runs, freqs - 1)),
        ],
        compiler_params=pltpu.CompilerParams(
            collective_id=0, has_side_effects=True, vmem_limit_bytes=VMEM_BYTES
        ),
    )(
        focus_direct[0],
        u_factors.reshape(col_tiles * 2 * RANK, receivers),
        v_factors.reshape(row_tiles * 2 * RANK, sources),
        tile_ranks[0],
        onset_rec,
        onset_src,
    )
    return plus[None], minus[None]


def fits(axes, focus_direct, u_factors, onset_rec):
    freqs, sides = axes["freq"], axes["src"]
    points, sources = focus_direct.shape[2:]
    receivers = u_factors.shape[-1]
    return (
        sides == 2
        and focus_direct.shape[0] == 1
        and freqs > 1
        and points % CHUNK == 0
        and onset_rec.shape[1] % (freqs * TILE) == 0
        and sources % (freqs * TILE) == 0
        and receivers % (sides * 2 * TILE) == 0
    )


def solution(mesh):
    placed = (
        P("freq", None, ("groups", "vp"), "src"),
        P("freq", "src", None, None, None),
        P("freq", None, None, None, "src"),
        P("freq", None, "src"),
        P(("groups", "vp"), "src"),
        P(("groups", "vp"), "src"),
    )
    axes = dict(mesh.shape)

    def part(focus_direct, u_factors, v_factors, tile_ranks, onset_rec, onset_src):
        args = (focus_direct, u_factors, v_factors, tile_ranks, onset_rec, onset_src)
        if fits(axes, focus_direct, u_factors, onset_rec):
            return whole_in_one(axes, *args)
        return per_device(*args)

    return jax.shard_map(
        part,
        mesh=mesh,
        in_specs=placed,
        out_specs=(
            P("freq", None, ("groups", "vp"), "src"),
            P("freq", None, ("groups", "vp"), "src"),
        ),
        check_vma=False,
    )
```

```python
import cmath
import functools
import math

import jax
import jax.numpy as jnp
from jax import lax
from jax.experimental import pallas as pl
from jax.experimental.pallas import tpu as pltpu
from jax.sharding import PartitionSpec as P

TILE = 256
RANK = 32
NT = 256
FLO = 8
ITERS = 2
CHUNK = 16
LANES = 128
VMEM_BYTES = 48 * 1024 * 1024


ORDER = (
    1, 0, 100, 200, 2, 102, 300, 202, 101, 400, 302, 201, 500, 301,
    402, 600, 502, 401, 602, 700, 501, 702, 802, 800, 10, 601, 12, 112,
    110, 210, 212, 310, 312, 410, 701, 412, 510, 801, 610, 512, 11, 612,
    710, 111, 211, 311, 712, 411, 812, 810, 22, 511, 20, 611, 711, 122,
    811, 21, 120, 121,
)


def make_tables(count):
    index = FLO + jnp.arange(count, dtype=jnp.int32)
    sample = jnp.arange(NT, dtype=jnp.int32)
    phase = (index[:, None] * sample[None, :] % NT).astype(jnp.float32) * (2.0 * math.pi / NT)
    cosine = jnp.cos(phase)
    sine = jnp.sin(phase)
    inverse = jnp.stack([cosine, -sine]) * (2.0 / NT)
    forward = jnp.stack([cosine, -sine])
    return (inverse, forward)


def window(spectrum, onset):
    inverse, forward = make_tables(spectrum.shape[0])
    signal = jnp.einsum("fcvm,cft->vmt", spectrum, inverse, precision=lax.Precision.HIGHEST)
    keep = jnp.arange(NT, dtype=jnp.int32)[None, None, :] < onset[:, :, None]
    signal = jnp.where(keep, signal, jnp.zeros_like(signal))
    return jnp.einsum("vmt,cft->fcvm", signal, forward, precision=lax.Precision.HIGHEST)


def coefficients(v_fac, mask, focus):
    points = focus.shape[1]
    row_tiles = v_fac.shape[0]
    col_tiles = v_fac.shape[-1] // TILE
    source = focus.reshape(2, points, col_tiles, TILE)
    v_tiles = v_fac.reshape(row_tiles, 2, RANK, col_tiles, TILE)
    form = "irjt,vjt->ivjr"
    z_real = jnp.einsum(
        form, v_tiles[:, 0], source[0], preferred_element_type=jnp.float32
    ) + jnp.einsum(form, v_tiles[:, 1], source[1], preferred_element_type=jnp.float32)
    z_imag = jnp.einsum(
        form, v_tiles[:, 0], source[1], preferred_element_type=jnp.float32
    ) - jnp.einsum(form, v_tiles[:, 1], source[0], preferred_element_type=jnp.float32)
    z_real = jnp.where(mask, z_real, 0.0).astype(jnp.bfloat16)
    z_imag = jnp.where(mask, z_imag, 0.0).astype(jnp.bfloat16)
    return jnp.stack([z_real, z_imag])


def expand_rows(u_fac, coeff):
    col_tiles = u_fac.shape[0]
    row_tiles = u_fac.shape[-1] // TILE
    points = coeff.shape[2]
    u_tiles = u_fac.reshape(col_tiles, 2, RANK, row_tiles, TILE)
    other = "jrit,ivjr->vit"
    y_real = jnp.einsum(
        other, u_tiles[:, 0], coeff[0], preferred_element_type=jnp.float32
    ) - jnp.einsum(other, u_tiles[:, 1], coeff[1], preferred_element_type=jnp.float32)
    y_imag = jnp.einsum(
        other, u_tiles[:, 0], coeff[1], preferred_element_type=jnp.float32
    ) + jnp.einsum(other, u_tiles[:, 1], coeff[0], preferred_element_type=jnp.float32)
    return jnp.stack([y_real.reshape(points, -1), y_imag.reshape(points, -1)])


def forward_local(u_fac, v_fac, mask, focus):
    return expand_rows(u_fac, coefficients(v_fac, mask, focus))


def adjoint_local(u_fac, v_fac, mask, focus):
    points = focus.shape[1]
    col_tiles = u_fac.shape[0]
    row_tiles = v_fac.shape[0]
    receiver = focus.reshape(2, points, row_tiles, TILE)
    v_tiles = v_fac.reshape(row_tiles, 2, RANK, col_tiles, TILE)
    u_tiles = u_fac.reshape(col_tiles, 2, RANK, row_tiles, TILE)
    form = "jrit,vit->ivjr"
    w_real = jnp.einsum(
        form, u_tiles[:, 0], receiver[0], preferred_element_type=jnp.float32
    ) + jnp.einsum(form, u_tiles[:, 1], receiver[1], preferred_element_type=jnp.float32)
    w_imag = jnp.einsum(
        form, u_tiles[:, 0], receiver[1], preferred_element_type=jnp.float32
    ) - jnp.einsum(form, u_tiles[:, 1], receiver[0], preferred_element_type=jnp.float32)
    w_real = jnp.where(mask, w_real, 0.0).astype(jnp.bfloat16)
    w_imag = jnp.where(mask, w_imag, 0.0).astype(jnp.bfloat16)
    other = "irjt,ivjr->vjt"
    x_real = jnp.einsum(
        other, v_tiles[:, 0], w_real, preferred_element_type=jnp.float32
    ) - jnp.einsum(other, v_tiles[:, 1], w_imag, preferred_element_type=jnp.float32)
    x_imag = jnp.einsum(
        other, v_tiles[:, 0], w_imag, preferred_element_type=jnp.float32
    ) + jnp.einsum(other, v_tiles[:, 1], w_real, preferred_element_type=jnp.float32)
    return jnp.stack([x_real.reshape(points, -1), x_imag.reshape(points, -1)])


def per_device(focus_direct, u_factors, v_factors, tile_ranks, onset_rec, onset_src):
    freq_count = lax.axis_size("freq")
    rank_index = jnp.arange(RANK, dtype=jnp.int32)
    masks = (rank_index[None, None, None, :] < tile_ranks[:, :, :, None])[:, :, None]
    rec_block = onset_rec.shape[1]
    rec_piece = rec_block // freq_count
    src_piece = onset_src.shape[1] // freq_count
    freq_place = lax.axis_index("freq")
    rec_onset = lax.dynamic_slice_in_dim(onset_rec, freq_place * rec_piece, rec_piece, 1)
    src_onset = lax.dynamic_slice_in_dim(onset_src, freq_place * src_piece, src_piece, 1)
    plus = focus_direct
    minus = None
    for sweep in range(ITERS):
        partial_terms = jax.vmap(forward_local)(u_factors, v_factors, masks, plus)
        summed = lax.psum_scatter(
            partial_terms.astype(jnp.bfloat16), "src", scatter_dimension=3, tiled=True
        ).astype(jnp.float32)
        traces = lax.all_to_all(
            summed.astype(jnp.bfloat16), "freq", split_axis=3, concat_axis=0, tiled=True
        ).astype(summed.dtype)
        windowed = window(traces, rec_onset).astype(jnp.bfloat16)
        minus = lax.all_to_all(windowed, "freq", split_axis=0, concat_axis=3, tiled=True)
        minus_all = lax.all_gather(minus, "src", axis=3, tiled=True)
        adjoint = jax.vmap(adjoint_local)(u_factors, v_factors, masks, minus_all)
        source_traces = lax.all_to_all(
            adjoint.astype(jnp.bfloat16), "freq", split_axis=3, concat_axis=0, tiled=True
        ).astype(adjoint.dtype)
        src_windowed = window(source_traces, src_onset)
        returned = lax.all_to_all(
            src_windowed.astype(jnp.bfloat16), "freq", split_axis=0, concat_axis=3, tiled=True
        ).astype(src_windowed.dtype)
        plus = (focus_direct.astype(jnp.float32) + returned).astype(jnp.bfloat16)
    return (plus, minus)


def repeat(count, width, step):
    width = math.gcd(count, width)
    if count == width:
        for n in range(count):
            step(n)
        return

    def turn(n, carry):
        for t in range(width):
            step(n * width + t)
        return carry

    lax.fori_loop(0, count // width, turn, 0)


def lane_index(rows):
    return lax.broadcasted_iota(jnp.int32, (rows, LANES), 1)


def combine(x):
    half = x.shape[0] // 2
    lane = lane_index(x.shape[0])
    row = lax.broadcasted_iota(jnp.int32, x.shape, 0)
    first = (lane % (2 * RANK)) < RANK
    other = jnp.concatenate([x[half:], x[:half]], axis=0)
    moved = jnp.where(first, pltpu.roll(other, LANES - RANK, 1), pltpu.roll(other, RANK, 1))
    return jnp.where(first == (row < half), x + moved, x - moved)


def pair_up(a, b):
    low = lane_index(a.shape[0]) < 2 * RANK
    return (
        jnp.where(low, a, pltpu.roll(b, 2 * RANK, 1)),
        jnp.where(low, pltpu.roll(a, 2 * RANK, 1), b),
    )


def masked(x, rank_a, rank_b):
    lane = lane_index(x.shape[0])
    rank = jnp.where(lane < 2 * RANK, rank_a, rank_b)
    return jnp.where(lane % RANK < rank, x, 0.0).astype(jnp.bfloat16)


def times(a, b):
    return (a[0] * b[0] - a[1] * b[1], a[0] * b[1] + a[1] * b[0])


def window_terms(onset, count):
    samples = onset.astype(jnp.float32)
    angle = (samples - NT / 2) * (math.pi / NT)
    square = angle * angle

    def series(top):
        total = jnp.full_like(square, 1.0)
        for n in range(top, 1, -2):
            total = 1.0 - square * total * (1.0 / (n * (n - 1)))
        return total

    sin_half = angle * series(13)
    cos_half = series(14)
    z = (sin_half * sin_half - cos_half * cos_half, -2.0 * sin_half * cos_half)
    powers = {1: z}

    def power(m):
        if m not in powers:
            low = m // 2 if m % 2 == 0 else m - 1
            powers[m] = times(power(low), power(m - low))
        return powers[m]

    def term(m):
        if m == 0:
            return (samples * (1.0 / NT), None)
        scale = 1.0 / (cmath.exp(2j * math.pi * m / NT) - 1.0) / NT
        re, im = power(m)
        re = re - 1.0
        return (re * scale.real - im * scale.imag, re * scale.imag + im * scale.real)

    return [term(m) for m in range(count)], [term(m) for m in range(2 * FLO, 2 * (FLO + count) - 1)]


def window_block(spectra, onset, count):
    diff, total = window_terms(onset, count)
    results = []
    for out in range(count):
        real = imag = None
        for f in range(count):
            x_re, x_im = spectra[f]
            s_re, s_im = total[f + out]
            d_re, d_im = diff[abs(f - out)]
            if d_im is None:
                a, b, c, d = d_re + s_re, -s_im, -s_im, d_re - s_re
            else:
                if f < out:
                    d_im = -d_im
                a, b, c, d = d_re + s_re, -(d_im + s_im), d_im - s_im, d_re - s_re
            one, two = x_re * a + x_im * b, x_re * c + x_im * d
            real = one if real is None else real + one
            imag = two if imag is None else imag + two
        results.append((real, imag))
    return results


NT_DOT = (((1,), (1,)), ((), ()))


def kernel(
    axes, focus_hbm, u_hbm, v_hbm, ranks_hbm, onset_rec_hbm, onset_src_hbm, plus_hbm, minus_hbm,
    ranks, focus, u_fac, v_fac, onset_rec, onset_src, plus, coeff, back, kept,
    x_out, x_in, a_out, a_in, b_out, b_in, d_in, g_out, g_in, h_out, h_in,
    load_sem, store_sem, x_sems, d_sems, a_sems, b_sems, g_sems, h_sems,
):
    freqs, sides = axes["freq"], axes["src"]
    here = lax.axis_index("freq")
    side = lax.axis_index("src")
    partner = 1 - side
    points = focus.shape[1]
    chunks = points // CHUNK
    row_tiles = u_fac.shape[1] // TILE
    col_tiles = v_fac.shape[1] // TILE
    half = row_tiles // sides
    rec_piece = onset_rec.shape[1]
    src_piece = onset_src.shape[1]
    tiles_each = src_piece // TILE
    src_half = src_piece // 2
    tiles_half = tiles_each // 2
    pairs_half = tiles_half // 2

    loads = [
        pltpu.make_async_copy(focus_hbm, focus, load_sem.at[0]),
        pltpu.make_async_copy(ranks_hbm, ranks, load_sem.at[5]),
        pltpu.make_async_copy(v_hbm, v_fac, load_sem.at[1]),
        pltpu.make_async_copy(u_hbm, u_fac, load_sem.at[2]),
        pltpu.make_async_copy(
            onset_rec_hbm.at[:, pl.ds(pl.multiple_of(here * rec_piece, LANES), rec_piece)], onset_rec, load_sem.at[3]
        ),
        pltpu.make_async_copy(
            onset_src_hbm.at[:, pl.ds(pl.multiple_of(here * src_piece, LANES), src_piece)], onset_src, load_sem.at[4]
        ),
    ]
    for load in loads:
        load.start()

    barrier = pltpu.get_barrier_semaphore()
    for step in range(1, freqs):
        pl.semaphore_signal(
            barrier, inc=1, device_id={"freq": lax.rem(here + step, freqs)}, device_id_type=pl.DeviceIdType.MESH
        )
    pl.semaphore_signal(barrier, inc=1, device_id={"src": partner}, device_id_type=pl.DeviceIdType.MESH)

    sends = []
    stores = []

    waited = set()

    def need(n):
        if n in waited:
            return
        waited.add(n)
        if n < len(loads):
            loads[n].wait()
        else:
            pl.semaphore_wait(barrier, freqs)

    def columns(index, size=TILE):
        if isinstance(index, int):
            return pl.ds(index * size, size)
        return pl.ds(pl.multiple_of(index * size, size), size)

    def across(source, target, sems, k):
        return pltpu.make_async_remote_copy(
            src_ref=source, dst_ref=target, send_sem=sems.at[0, k], recv_sem=sems.at[1, k],
            device_id={"src": partner}, device_id_type=pl.DeviceIdType.MESH,
        )

    def along(out, into, sems, k, step):
        target = lax.rem(here + step, freqs)
        return pltpu.make_async_remote_copy(
            src_ref=out.at[k, target], dst_ref=into.at[k, here],
            send_sem=sems.at[0, k, step - 1], recv_sem=sems.at[1, k, step - 1],
            device_id={"freq": target}, device_id_type=pl.DeviceIdType.MESH,
        )

    def arrived(out, into, sems, k, step):
        source = lax.rem(here + freqs - step, freqs)
        pltpu.make_async_remote_copy(
            src_ref=out.at[k, source], dst_ref=into.at[k, source],
            send_sem=sems.at[0, k, step - 1], recv_sem=sems.at[1, k, step - 1],
            device_id={"freq": source}, device_id_type=pl.DeviceIdType.MESH,
        ).wait_recv()

    def send(copy):
        copy.start()
        sends.append(copy)

    def spread_out(first, second, store):
        for q in range(first.shape[1] // LANES):
            lanes = slice(q * LANES, (q + 1) * LANES)
            even, odd = pair_up(combine(first[:, lanes]), combine(second[:, lanes]))
            store(2 * q, even)
            store(2 * q + 1, odd)

    def collect(sweep, c, part):
        rows = slice(c * CHUNK, (c + 1) * CHUNK)
        if sweep > 0:
            k = 2 * ((sweep - 1) * chunks + c) + part
            for step in range(1, freqs):
                arrived(h_out, h_in, h_sems, k, step)
            for q in range(freqs):
                lanes = pl.ds(q * src_piece + part * src_half, src_half)
                start = focus[:, rows, lanes].reshape(2 * CHUNK, src_half).astype(jnp.float32)
                plus[(sweep - 1) * chunks + c, :, lanes] = (start + h_in[k, q].astype(jnp.float32)).astype(jnp.bfloat16)
        if sweep == ITERS:
            if part == 1:
                for side_of in range(2):
                    store = pltpu.make_async_copy(
                        plus.at[(sweep - 1) * chunks + c, pl.ds(side_of * CHUNK, CHUNK), :],
                        plus_hbm.at[side_of, pl.ds(c * CHUNK, CHUNK), :],
                        store_sem.at[0, c, side_of],
                    )
                    store.start()
                    stores.append(store)
            return
        for q in range(freqs):
            for n in range(pairs_half):
                pair = (q * src_piece + part * src_half) // (2 * TILE) + n
                products = []
                for t in range(2):
                    cols = columns(2 * pair + t)
                    if sweep == 0:
                        block = focus[:, rows, cols].reshape(2 * CHUNK, TILE)
                    else:
                        block = plus[(sweep - 1) * chunks + c, :, cols]
                    products.append(lax.dot_general(block, v_fac[:, cols], NT_DOT, preferred_element_type=jnp.float32))

                def store(i, value):
                    coeff[c, i, :, columns(pair, LANES)] = masked(value, ranks[i, 2 * pair], ranks[i, 2 * pair + 1])

                spread_out(products[0], products[1], store)

    def forward(sweep, c):
        k = sweep * chunks + c
        need(3)

        def product(i):
            return jnp.dot(coeff[c, i], u_fac[:, columns(i)], preferred_element_type=jnp.float32)

        for n in range(half):
            x_out[k, :, columns(n)] = product(partner * half + n).astype(jnp.bfloat16)
        need(6)
        send(across(x_out.at[k], x_in.at[k], x_sems, k))
        for n in range(half):
            kept[c, :, columns(n)] = product(side * half + n)

    def reduce(sweep, c):
        k = sweep * chunks + c
        across(x_out.at[k], x_in.at[k], x_sems, k).wait_recv()
        for q in range(freqs):
            lanes = slice(q * rec_piece, (q + 1) * rec_piece)
            a_out[k, q] = (kept[c, :, lanes] + x_in[k, :, lanes].astype(jnp.float32)).astype(jnp.bfloat16)
        for step in range(1, freqs):
            send(along(a_out, a_in, a_sems, k, step))
        a_in[k, here] = a_out[k, here]

    def window(k, c, from_ref, to_ref, onset, first, size):
        rows = slice(c * CHUNK, (c + 1) * CHUNK)

        def one(n):
            lanes = columns(n, LANES)
            spectra = []
            for f in range(freqs):
                both = from_ref[k, f, :, lanes].astype(jnp.float32)
                spectra.append((both[:CHUNK], both[CHUNK:]))
            for f, (real, imag) in enumerate(window_block(spectra, onset[rows, columns(n + first // LANES, LANES)], freqs)):
                to_ref[k, f, :, lanes] = jnp.concatenate([real, imag], axis=0).astype(jnp.bfloat16)

        repeat(size // LANES, 2, one)

    def window_rec(sweep, c):
        k = sweep * chunks + c
        need(4)
        for step in range(1, freqs):
            arrived(a_out, a_in, a_sems, k, step)
        window(k, c, a_in, b_out, onset_rec, 0, rec_piece)
        for step in range(1, freqs):
            send(along(b_out, b_in, b_sems, k, step))
        b_in[k, here] = b_out[k, here]

    def spread(sweep, c):
        k = sweep * chunks + c
        for step in range(1, freqs):
            arrived(b_out, b_in, b_sems, k, step)
        send(across(b_in.at[k], d_in.at[k], d_sems, k))
        if sweep == ITERS - 1:
            for part in range(2):
                for q in range(freqs):
                    store = pltpu.make_async_copy(
                        b_in.at[k, q, pl.ds(part * CHUNK, CHUNK), :],
                        minus_hbm.at[part, pl.ds(c * CHUNK, CHUNK), pl.ds(q * rec_piece, rec_piece)],
                        store_sem.at[1, c, part * freqs + q],
                    )
                    store.start()
                    stores.append(store)

    def adjoint(sweep, c):
        k = sweep * chunks + c

        def back_pairs(source, first_tile):
            def one(pair):
                products = []
                for t in range(2):
                    n = 2 * pair + t
                    block = source[k, n * TILE // rec_piece, :, pl.ds(pl.multiple_of(n * TILE % rec_piece, LANES), TILE)]
                    products.append(
                        lax.dot_general(
                            block, u_fac[:, columns(first_tile + n)], NT_DOT, preferred_element_type=jnp.float32
                        )
                    )
                at = first_tile // 2 + pair

                def store(j, value):
                    back[j, :, columns(at, LANES)] = masked(value, ranks[2 * at, j], ranks[2 * at + 1, j])

                spread_out(products[0], products[1], store)

            repeat(half // 2, 2, one)

        back_pairs(b_in, side * half)
        across(b_in.at[k], d_in.at[k], d_sems, k).wait_recv()
        back_pairs(d_in, partner * half)

        for part in range(2):
            for step in list(range(1, freqs)) + [0]:
                target = lax.rem(here + step, freqs)
                for n in range(tiles_half):
                    j = target * tiles_each + part * tiles_half + n
                    value = jnp.dot(back[j], v_fac[:, columns(j)], preferred_element_type=jnp.float32)
                    value = value.astype(jnp.bfloat16)
                    if step == 0:
                        g_in[2 * k + part, here, :, columns(n)] = value
                    else:
                        g_out[2 * k + part, target, :, columns(n)] = value
                if step > 0:
                    send(along(g_out, g_in, g_sems, 2 * k + part, step))

    def window_src(sweep, c, part):
        k = 2 * (sweep * chunks + c) + part
        need(5)
        for step in range(1, freqs):
            arrived(g_out, g_in, g_sems, k, step)
        window(k, c, g_in, h_out, onset_src, part * src_half, src_half)
        for step in range(1, freqs):
            send(along(h_out, h_in, h_sems, k, step))
        h_in[k, here] = h_out[k, here]

    for n in range(3):
        need(n)
    stages = [
        functools.partial(collect, part=0), functools.partial(collect, part=1), forward, reduce, window_rec, spread,
        adjoint, functools.partial(window_src, part=0), functools.partial(window_src, part=1),
    ]
    for stage, sweep, c in order_of(chunks):
        stages[stage](sweep, c)
    for copy in sends:
        copy.wait_send()
    for store in stores:
        store.wait()


def order_of(chunks):
    if chunks == 3:
        return [(code // 100, code // 10 % 10, code % 10) for code in ORDER]
    whole = [(stage, sweep, c) for sweep in range(ITERS) for stage in range(9) for c in range(chunks)]
    return whole + [(stage, ITERS, c) for stage in range(2) for c in range(chunks)]


def whole_in_one(axes, focus_direct, u_factors, v_factors, tile_ranks, onset_rec, onset_src):
    freqs = axes["freq"]
    points, sources = focus_direct.shape[2:]
    receivers = u_factors.shape[-1]
    block = onset_rec.shape[1]
    rec_piece, src_piece = block // freqs, sources // freqs
    row_tiles, col_tiles = receivers // TILE, sources // TILE
    chunks = points // CHUNK
    runs = ITERS * chunks
    rows = 2 * CHUNK
    bf16, f32 = jnp.bfloat16, jnp.float32
    small = pltpu.VMEM((runs, freqs, rows, rec_piece), bf16)
    large = pltpu.VMEM((2 * runs, freqs, rows, src_piece // 2), bf16)
    dma = pltpu.SemaphoreType.DMA
    anywhere = pl.BlockSpec(memory_space=pl.ANY)
    plus, minus = pl.pallas_call(
        functools.partial(kernel, axes),
        out_shape=(
            jax.ShapeDtypeStruct((2, points, sources), bf16),
            jax.ShapeDtypeStruct((2, points, block), bf16),
        ),
        in_specs=[pl.BlockSpec(memory_space=pltpu.HBM)] * 6,
        out_specs=(anywhere, anywhere),
        scratch_shapes=[
            pltpu.SMEM((row_tiles, col_tiles), jnp.int32),
            pltpu.VMEM((2, points, sources), bf16),
            pltpu.VMEM((col_tiles * 2 * RANK, receivers), bf16),
            pltpu.VMEM((row_tiles * 2 * RANK, sources), bf16),
            pltpu.VMEM((points, rec_piece), jnp.int32),
            pltpu.VMEM((points, src_piece), jnp.int32),
            pltpu.VMEM((2 * chunks, rows, sources), bf16),
            pltpu.VMEM((chunks, row_tiles, rows, col_tiles * 2 * RANK), bf16),
            pltpu.VMEM((col_tiles, rows, row_tiles * 2 * RANK), bf16),
            pltpu.VMEM((chunks, rows, block), f32),
            pltpu.VMEM((runs, rows, block), bf16),
            pltpu.VMEM((runs, rows, block), bf16),
            small, small, small, small, small,
            large, large, large, large,
            dma((6,)),
            dma((2, chunks, 2 * freqs)),
            dma((2, runs)),
            dma((2, runs)),
            dma((2, runs, freqs - 1)),
            dma((2, runs, freqs - 1)),
            dma((2, 2 * runs, freqs - 1)),
            dma((2, 2 * runs, freqs - 1)),
        ],
        compiler_params=pltpu.CompilerParams(
            collective_id=0, has_side_effects=True, vmem_limit_bytes=VMEM_BYTES
        ),
    )(
        focus_direct[0],
        u_factors.reshape(col_tiles * 2 * RANK, receivers),
        v_factors.reshape(row_tiles * 2 * RANK, sources),
        tile_ranks[0],
        onset_rec,
        onset_src,
    )
    return plus[None], minus[None]


def fits(axes, focus_direct, u_factors, onset_rec):
    freqs, sides = axes["freq"], axes["src"]
    points, sources = focus_direct.shape[2:]
    receivers = u_factors.shape[-1]
    return (
        sides == 2
        and focus_direct.shape[0] == 1
        and freqs > 1
        and points % CHUNK == 0
        and onset_rec.shape[1] % (freqs * TILE) == 0
        and sources % (freqs * 4 * TILE) == 0
        and receivers % (sides * 2 * TILE) == 0
    )


def solution(mesh):
    placed = (
        P("freq", None, ("groups", "vp"), "src"),
        P("freq", "src", None, None, None),
        P("freq", None, None, None, "src"),
        P("freq", None, "src"),
        P(("groups", "vp"), "src"),
        P(("groups", "vp"), "src"),
    )
    axes = dict(mesh.shape)

    def part(focus_direct, u_factors, v_factors, tile_ranks, onset_rec, onset_src):
        args = (focus_direct, u_factors, v_factors, tile_ranks, onset_rec, onset_src)
        if fits(axes, focus_direct, u_factors, onset_rec):
            return whole_in_one(axes, *args)
        return per_device(*args)

    return jax.shard_map(
        part,
        mesh=mesh,
        in_specs=placed,
        out_specs=(
            P("freq", None, ("groups", "vp"), "src"),
            P("freq", None, ("groups", "vp"), "src"),
        ),
        check_vma=False,
    )
```
